128 devices in a mesh: group: 8 (over x, core), member: 16 (over y, z).
Axes of the slice: x: 4, y: 4, z: 4, core: 2. Of those that a mesh axis runs over, the one named last changes fastest.
Arguments:
- amplitudes: bfloat16 [512, 512, 128], P(('group', 'member')), may hold values from -6 to 6
- integrals: bfloat16 [28672, 128, 128], P(('group', 'member')), may hold values from -0.0625 to 0.0625
- task_plan: int32 [28672, 3], P(('group', 'member')), may hold values from 0 to 511, as said below
Outputs:
- residual_tiles: float32 [512, 512, 128], P(('group', 'member'))
The draws below stay inside these ranges and needn't reach their ends.
Inputs may be any that keep to these rules, and one draw needn't show every extreme that they name: `task_plan`: column 0 is the source tile, column 1 the destination tile, column 2 the executing device as index in the order group, then member. Both tiles of a row lie in the same symmetry block of 64 consecutive tiles, and the executor is a device of the group that holds that block. Every device is the executor of exactly 224 rows. The rows of one device name one executor at most 2 times, and name destination tiles held by one device at most 4 times; both bounds are reached in every draw.
All inputs are finite; a program needn't handle non-finite values.
Results may differ from the reference program's by a relative error of at most 0.0003.
Values may be sent and summed in bfloat16 or wider, within the bound.
A program may use at most 192 MiB of HBM per device.

```python
import math
import jax
import jax.numpy as jnp
from jax import lax

W = 128
ROWS = 512
TILE_DEV = 4
TASK_DEV = 224
NTILE = 512
NTASK = 28672
N_GROUP = 8
N_MEMBER = 16


def draw_task_plan(key, part):
    devices_all = N_GROUP * N_MEMBER
    base = TASK_DEV // devices_all
    extra = TASK_DEV - base * devices_all
    peer_most = (TASK_DEV + devices_all - 1) // devices_all
    dest_most = 2 * peer_most
    keys = jax.random.split(jax.random.fold_in(key, 41), 7)
    first_perm = jax.random.permutation(keys[0], devices_all).astype(jnp.int32)
    second_perm = jax.random.permutation(keys[1], devices_all).astype(jnp.int32)
    senders = jnp.arange(devices_all, dtype=jnp.int32)
    counts = base + ((first_perm[None, :] - second_perm[:, None]) % devices_all < extra).astype(jnp.int32)
    slots = devices_all * peer_most
    copies = jnp.arange(slots, dtype=jnp.int32) % peer_most
    slot_exec = jnp.arange(slots, dtype=jnp.int32) // peer_most
    used = copies[None, :] < counts[:, slot_exec]
    noise = jax.random.randint(keys[2], (devices_all, slots), 0, 1 << 20, dtype=jnp.int32)
    score = (noise + jnp.where(used, 0, 1 << 20)) * slots + jnp.arange(slots, dtype=jnp.int32)[None, :]
    chosen = jnp.argsort(score, axis=1)[:, :TASK_DEV].astype(jnp.int32)
    executor = chosen // peer_most
    sym_block = executor // N_MEMBER
    onehot = (sym_block[:, :, None] == jnp.arange(N_GROUP, dtype=jnp.int32)[None, None, :]).astype(jnp.int32)
    rank = jnp.sum(jnp.cumsum(onehot, axis=1) * onehot, axis=2) - 1
    hot_member = jax.random.randint(keys[3], (N_GROUP,), 0, N_MEMBER, dtype=jnp.int32)
    member_ids = jnp.arange(N_MEMBER, dtype=jnp.int32)
    mixed = jax.random.randint(keys[4], (devices_all, N_GROUP, N_MEMBER), 0, 1 << 20, dtype=jnp.int32) * N_MEMBER + member_ids[None, None, :]
    mixed = jnp.where(member_ids[None, None, :] == hot_member[None, :, None], 1 << 30, mixed)
    others = jnp.argsort(mixed, axis=2).astype(jnp.int32)
    later = jnp.maximum(rank - dest_most, 0) % (N_MEMBER - 1)
    other_owner = others[senders[:, None], sym_block, later]
    owner = jnp.where(rank < dest_most, hot_member[sym_block], other_owner)
    within = jax.random.randint(keys[5], (devices_all, TASK_DEV), 0, TILE_DEV, dtype=jnp.int32)
    destination = (sym_block * N_MEMBER + owner) * TILE_DEV + within
    source = sym_block * (TILE_DEV * N_MEMBER) + jax.random.randint(keys[6], (devices_all, TASK_DEV), 0, TILE_DEV * N_MEMBER, dtype=jnp.int32)
    return jnp.stack([source, destination, executor], axis=-1).reshape(devices_all * TASK_DEV, 3).astype(jnp.int32)


def block_levels(own_key, dims, cuts, smallest, largest):
    loudness, own = 1.0, jax.random.fold_in(own_key, 6)
    for position, shards_of in cuts:
        heights = jnp.exp(jax.random.uniform(jax.random.fold_in(own, position), (shards_of,), jnp.float32, smallest / len(cuts), largest / len(cuts)))
        loudness = loudness * jnp.repeat(heights, dims[position] // shards_of).reshape([-1 if axis == position else 1 for axis in range(len(dims))])
    return loudness


def normal_values(stream_key, dims, spread, reach, cuts=(), kind=jnp.bfloat16):
    result = spread * jax.random.normal(stream_key, dims, jnp.float32)
    if cuts:
        result = result * block_levels(stream_key, dims, cuts, -0.22, 0.18)
    return jnp.clip(result, -reach, reach).astype(kind)


def setup_inputs(seed: int = 0) -> dict:
    key_list = jax.random.split(jax.random.key(seed), 4)
    amplitudes = normal_values(key_list[0], (NTILE, ROWS, W), 1.0, 6.0, ((0, 128),))
    integrals = normal_values(key_list[1], (NTASK, W, W), (W * TASK_DEV // TILE_DEV) ** -0.5, 0.0625, ((0, 128),))
    task_plan = draw_task_plan(jax.random.fold_in(key_list[3], 71), 0)
    return dict(amplitudes=amplitudes, integrals=integrals, task_plan=task_plan)


def reference(amplitudes, integrals, task_plan):
    count = integrals.shape[0]
    block = math.gcd(count, 256)
    turns = count // block
    width = integrals.shape[-1]
    rows = amplitudes.shape[1]
    source = task_plan[:, 0].reshape(turns, block)
    target = task_plan[:, 1].reshape(turns, block)
    tiles = integrals.reshape(turns, block, width, width)

    def advance(total, pieces):
        piece_tiles, piece_source, piece_target = pieces
        left_rows = jnp.take(amplitudes, piece_source, axis=0).astype(jnp.float32)
        product = jnp.einsum("brw,bwv->brv", left_rows, piece_tiles.astype(jnp.float32),
                             precision=lax.Precision.HIGHEST)
        return total.at[piece_target].add(product), None

    start_total = jnp.zeros((amplitudes.shape[0], rows, width), jnp.float32)
    total, unused = lax.scan(advance, start_total, (tiles, source, target))
    return total
```

```python
import jax
import jax.numpy as jnp
from jax import lax
from jax.experimental import pallas as pl
from jax.experimental.pallas import tpu as pltpu
from jax.sharding import PartitionSpec as P

MESH = pl.DeviceIdType.MESH
ANY = pl.BlockSpec(memory_space=pl.ANY)
VMEM = pl.BlockSpec(memory_space=pltpu.VMEM)
SMEM = pl.BlockSpec(memory_space=pltpu.SMEM)

NX, NC, NY, NZ = 4, 2, 4, 4
GROUPS = NX * NC
MEMBERS = NY * NZ
CAP = 32
TILES = 4
BLOCK = MEMBERS * TILES
W = 128
ROWS = 512
CODED = ROWS + 16


def position():
    group = lax.axis_index("group")
    member = lax.axis_index("member")
    return group // NC, lax.rem(group, NC), member // NZ, lax.rem(member, NZ)


def device(x, core, y, z):
    return (x * NC + core, y * NZ + z)


def wrap(value, size):
    return lax.rem(value + size, size)


def send(src, dst, send_sem, recv_sem, target):
    copy = pltpu.make_async_remote_copy(
        src_ref=src, dst_ref=dst, send_sem=send_sem, recv_sem=recv_sem,
        device_id=target, device_id_type=MESH,
    )
    copy.start()
    return copy


def greet(targets):
    barrier = pltpu.get_barrier_semaphore()
    for target in targets:
        pl.semaphore_signal(barrier, inc=1, device_id=target, device_id_type=MESH)
    pl.semaphore_wait(barrier, len(targets))


PEERS = ((1, 0), (3, 0), (2, 0), (1, 1), (3, 1), (2, 1), (0, 1))


def exchange_kernel(
    order, labels, integrals, amps, tiles_out, labels_out, amps_out,
    outgoing, tile_send, tile_recv, label_send, label_recv, amp_send, amp_recv, local_sem,
):
    x, core, y, z = position()
    group = x * NC + core
    member = y * NZ + z

    def across(dx, dc):
        return device(wrap(x + dx, NX), wrap(core + dc, NC), y, z)

    def along(axis, step):
        if axis == 0:
            return device(x, core, wrap(y + step, NY), z)
        return device(x, core, y, wrap(z + step, NZ))

    greet([across(*p) for p in PEERS] + [along(a, s) for a in (0, 1) for s in (1, 2, 3)])

    waits = []
    own = [
        pltpu.make_async_copy(amps, amps_out.at[member], local_sem.at[0]),
        pltpu.make_async_copy(labels.at[group], labels_out.at[group], local_sem.at[1]),
    ]
    for copy in own:
        copy.start()
    first = {}
    count = 0
    for axis in (0, 1):
        half = pl.ds(axis * 2, 2)
        for step in (1, 3, 2):
            first[axis, step] = send(
                amps.at[half], amps_out.at[member, half], amp_send.at[count], amp_recv.at[count], along(axis, step)
            )
            count += 1

    def gather(slot, target):
        @pl.loop(0, CAP)
        def _(t):
            outgoing[slot, t] = integrals[order[target * CAP + t]]

    for k, (dx, dc) in enumerate(PEERS):
        target = wrap(x + dx, NX) * NC + wrap(core + dc, NC)
        gather(k, target)
        waits.append(send(outgoing.at[k], tiles_out.at[group], tile_send.at[k], tile_recv.at[k], across(dx, dc)))
        waits.append(send(labels.at[target], labels_out.at[group], label_send.at[k], label_recv.at[k], across(dx, dc)))
    gather(7, group)
    mine = pltpu.make_async_copy(outgoing.at[7], tiles_out.at[group], local_sem.at[2])
    mine.start()
    own.append(mine)

    for arrived in (0, 1, 3, 2):
        for axis in (0, 1):
            half = pl.ds(axis * 2, 2)
            if arrived == 0:
                where, source = member, amps.at[half]
            else:
                first[axis, arrived].wait_recv()
                back = 4 - arrived
                where = wrap(y + back, NY) * NZ + z if axis == 0 else y * NZ + wrap(z + back, NZ)
                source = amps_out.at[where, half]
            for step in (1, 3, 2):
                waits.append(
                    send(source, amps_out.at[where, half], amp_send.at[count], amp_recv.at[count], along(1 - axis, step))
                )
                count += 1
    for copy in first.values():
        copy.wait_send()
    for copy in own:
        copy.wait()
    for copy in waits:
        copy.wait()


def exchange(order, labels, integrals, amps):
    return pl.pallas_call(
        exchange_kernel,
        out_shape=(
            jax.ShapeDtypeStruct((GROUPS, CAP, W, W), jnp.bfloat16),
            jax.ShapeDtypeStruct((GROUPS, 8, 128), jnp.int32),
            jax.ShapeDtypeStruct((MEMBERS, TILES, ROWS, W), jnp.bfloat16),
        ),
        in_specs=[SMEM, ANY, VMEM, ANY],
        out_specs=(ANY, ANY, ANY),
        scratch_shapes=[
            pltpu.VMEM((8, CAP, W, W), jnp.bfloat16),
            pltpu.SemaphoreType.DMA((7,)),
            pltpu.SemaphoreType.DMA((7,)),
            pltpu.SemaphoreType.DMA((7,)),
            pltpu.SemaphoreType.DMA((7,)),
            pltpu.SemaphoreType.DMA((30,)),
            pltpu.SemaphoreType.DMA((30,)),
            pltpu.SemaphoreType.DMA((3,)),
        ],
        compiler_params=pltpu.CompilerParams(collective_id=0, has_side_effects=True, vmem_limit_bytes=40 << 20),
        name="exchange",
    )(order, labels, integrals, amps)


def encode(value):
    most = jnp.max(jnp.abs(value.reshape(ROWS // 16, 16, W)), axis=0)
    power = jnp.ceil(jnp.log2(jnp.maximum(most, 1e-30)) - 14.999)
    factor = jnp.exp2(-power)
    whole = jnp.round(value.reshape(ROWS // 16, 16, W) * factor[None]).astype(jnp.int32)
    return whole.reshape(ROWS, W).astype(jnp.int16), power.astype(jnp.int32).astype(jnp.int16)


def decode(ref):
    factor = jnp.exp2(ref[pl.ds(ROWS, 16), :].astype(jnp.int32).astype(jnp.float32))
    whole = ref[pl.ds(0, ROWS), :].astype(jnp.int32).astype(jnp.float32)
    return (whole.reshape(ROWS // 16, 16, W) * factor[None]).reshape(ROWS, W)


def write(ref, value):
    whole, power = encode(value)
    ref[pl.ds(0, ROWS), :] = whole
    ref[pl.ds(ROWS, 16), :] = power


def contract_kernel(labels, tiles, amps, out, head, following, total):
    step = pl.program_id(0)

    @pl.when(step == 0)
    def _():
        @pl.loop(0, BLOCK)
        def _(a):
            head[a] = -1

        @pl.loop(0, GROUPS * CAP)
        def _(s):
            label = labels[s // CAP, 0, lax.rem(s, CAP)]

            @pl.when(label > 0)
            def _():
                a = lax.rem(label - 1, BLOCK)
                following[s] = head[a]
                head[a] = s

    half, low, first, second = step // 32, lax.rem(step // 16, 2), lax.rem(step // 4, 4), lax.rem(step, 4)
    owner = jnp.where(half == 0, first * NZ + second, second * NZ + first)
    a = owner * TILES + half * 2 + low

    def source(s):
        return (labels[s // CAP, 0, lax.rem(s, CAP)] - 1) // BLOCK

    total[...] = jnp.zeros_like(total)

    def pair(s):
        t = following[s]

        @pl.when(t < 0)
        def _():
            total[...] += jnp.dot(amps[source(s)], tiles[s], preferred_element_type=jnp.float32)

        @pl.when(t >= 0)
        def _():
            left = jnp.concatenate([amps[source(s)], amps[source(t)]], axis=1)
            right = jnp.concatenate([tiles[s], tiles[t]], axis=0)
            total[...] += jnp.dot(left, right, preferred_element_type=jnp.float32)

        return jnp.where(t < 0, -1, following[jnp.maximum(t, 0)])

    lax.while_loop(lambda s: s >= 0, pair, head[a])
    write(out.at[0], total[...])


def contract(labels, tiles, amps):
    return pl.pallas_call(
        contract_kernel,
        grid=(BLOCK,),
        out_shape=jax.ShapeDtypeStruct((BLOCK, CODED, W), jnp.int16),
        in_specs=[SMEM, VMEM, VMEM],
        out_specs=pl.BlockSpec((1, CODED, W), lambda i: (i, 0, 0)),
        scratch_shapes=[
            pltpu.SMEM((BLOCK,), jnp.int32),
            pltpu.SMEM((GROUPS * CAP,), jnp.int32),
            pltpu.VMEM((ROWS, W), jnp.float32),
        ],
        compiler_params=pltpu.CompilerParams(vmem_limit_bytes=40 << 20),
        name="contract",
    )(labels, tiles.reshape(GROUPS * CAP, W, W), amps.reshape(BLOCK, ROWS, W))


CASES = tuple((h, w) for h in (0, 1) for w in (0, 1))


def scatter_kernel(
    parts, out, held, a_in, b_in, c_out, c_in, summed, coded, d_in, e_in, f_out, f_in,
    held_sem, a_send, a_recv, b_send, b_recv, c_send, c_recv, d_send, d_recv, e_send, e_recv, f_send, f_recv,
):
    x, core, y, z = position()
    at = (y, z)

    def along(axis, step):
        if axis == 0:
            return device(x, core, wrap(y + step, NY), z)
        return device(x, core, y, wrap(z + step, NZ))

    def second_of(h, w, k):
        sense = 1 - 2 * w
        return wrap(at[1 - h] + (2, -sense, sense, 0)[k], 4)

    greet([along(a, s) for a in (0, 1) for s in (1, 3)])
    loads, a_copy, b_copy, c_copy, d_copy, e_copy, f_copy = {}, {}, {}, {}, {}, {}, {}
    for k in range(4):
        for i, (h, w) in enumerate(CASES):
            sense = 1 - 2 * w
            a_copy[i, k] = send(
                parts.at[h, w, wrap(at[h] + 2, 4), second_of(h, w, k)], a_in.at[i, k],
                a_send.at[i, k], a_recv.at[i, k], along(h, sense),
            )
    for i, (h, w) in enumerate(CASES):
        sense = 1 - 2 * w
        for j, p in enumerate((wrap(at[h] + sense, 4), at[h])):
            loads[i, j] = pltpu.make_async_copy(parts.at[h, w, p], held.at[i, j], held_sem.at[i, j])
            loads[i, j].start()
        b_copy[i] = send(
            parts.at[h, w, wrap(at[h] - sense, 4)], b_in.at[i], b_send.at[i], b_recv.at[i], along(h, -sense)
        )
    for i in range(4):
        loads[i, 0].wait()
    for k in range(4):
        for i, (h, w) in enumerate(CASES):
            sense = 1 - 2 * w
            a_copy[i, k].wait()
            write(c_out.at[i, k], decode(a_in.at[i, k]) + decode(held.at[i, 0, second_of(h, w, k)]))
            c_copy[i, k] = send(
                c_out.at[i, k], c_in.at[i, k], c_send.at[i, k], c_recv.at[i, k], along(h, sense)
            )
    for i in range(4):
        loads[i, 1].wait()
        b_copy[i].wait()
    for k in range(4):
        for i, (h, w) in enumerate(CASES):
            sense = 1 - 2 * w
            q = second_of(h, w, k)
            c_copy[i, k].wait()
            value = decode(c_in.at[i, k]) + decode(held.at[i, 1, q]) + decode(b_in.at[i, q])
            if k == 0:
                write(coded.at[i, 0], value)
                d_copy[i] = send(coded.at[i, 0], d_in.at[i], d_send.at[i], d_recv.at[i], along(1 - h, sense))
            elif k == 1:
                write(coded.at[i, 1], value)
                e_copy[i] = send(coded.at[i, 1], e_in.at[i], e_send.at[i], e_recv.at[i], along(1 - h, -sense))
            else:
                summed[i, k - 2] = value
    for i, (h, w) in enumerate(CASES):
        sense = 1 - 2 * w
        d_copy[i].wait()
        write(f_out.at[i], decode(d_in.at[i]) + summed[i, 0])
        f_copy[i] = send(f_out.at[i], f_in.at[i], f_send.at[i], f_recv.at[i], along(1 - h, sense))
    for i, (h, w) in enumerate(CASES):
        e_copy[i].wait()
        f_copy[i].wait()
        out[2 * h + w] = summed[i, 1] + decode(e_in.at[i]) + decode(f_in.at[i])


def scatter(parts):
    tile = (CODED, W)
    dma = pltpu.SemaphoreType.DMA
    return pl.pallas_call(
        scatter_kernel,
        out_shape=jax.ShapeDtypeStruct((TILES, ROWS, W), jnp.float32),
        in_specs=[ANY],
        out_specs=VMEM,
        scratch_shapes=[
            pltpu.VMEM((4, 2, 4) + tile, jnp.int16),
            pltpu.VMEM((4, 4) + tile, jnp.int16),
            pltpu.VMEM((4, 4) + tile, jnp.int16),
            pltpu.VMEM((4, 4) + tile, jnp.int16),
            pltpu.VMEM((4, 4) + tile, jnp.int16),
            pltpu.VMEM((4, 2, ROWS, W), jnp.float32),
            pltpu.VMEM((4, 2) + tile, jnp.int16),
            pltpu.VMEM((4,) + tile, jnp.int16),
            pltpu.VMEM((4,) + tile, jnp.int16),
            pltpu.VMEM((4,) + tile, jnp.int16),
            pltpu.VMEM((4,) + tile, jnp.int16),
            dma((4, 2)),
            dma((4, 4)), dma((4, 4)),
            dma((4,)), dma((4,)),
            dma((4, 4)), dma((4, 4)),
            dma((4,)), dma((4,)),
            dma((4,)), dma((4,)),
            dma((4,)), dma((4,)),
        ],
        compiler_params=pltpu.CompilerParams(collective_id=1, has_side_effects=True, vmem_limit_bytes=40 << 20),
        name="scatter",
    )(parts)


def slots(plan):
    rows = plan.shape[0]
    group = plan[:, 2] // MEMBERS
    row = jnp.arange(rows, dtype=jnp.int32)
    earlier = (group[None, :] == group[:, None]) & (row[None, :] < row[:, None])
    place = group * CAP + jnp.sum(earlier.astype(jnp.int32), axis=1)
    label = 1 + plan[:, 1] % BLOCK + BLOCK * (plan[:, 0] % BLOCK)
    here = jnp.arange(GROUPS * CAP, dtype=jnp.int32)[:, None] == place[None, :]
    order = jnp.sum(jnp.where(here, row[None, :], 0), axis=1)
    labels = jnp.sum(jnp.where(here, label[None, :], 0), axis=1)
    return order, jnp.pad(labels.reshape(GROUPS, 1, CAP), ((0, 0), (0, 7), (0, 128 - CAP)))


def on_device(amplitudes, integrals, task_plan):
    order, labels = slots(task_plan)
    tiles, labels, amps = exchange(order, labels, integrals, amplitudes)
    parts = contract(labels, tiles, amps)
    return scatter(parts.reshape(2, 2, 4, 4, CODED, W))


def solution(mesh):
    in_specs = (
        P(("group", "member"), None, None),
        P(("group", "member"), None, None),
        P(("group", "member"), None),
    )
    out_specs = P(("group", "member"), None, None)
    return jax.shard_map(
        on_device, mesh=mesh, in_specs=in_specs, out_specs=out_specs, check_vma=False
    )
```

```python
import jax
import jax.numpy as jnp
from jax import lax
from jax.experimental import pallas as pl
from jax.experimental.pallas import tpu as pltpu
from jax.sharding import PartitionSpec as P

MESH = pl.DeviceIdType.MESH
ANY = pl.BlockSpec(memory_space=pl.ANY)
VMEM = pl.BlockSpec(memory_space=pltpu.VMEM)
SMEM = pl.BlockSpec(memory_space=pltpu.SMEM)

NX, NC, NY, NZ = 4, 2, 4, 4
GROUPS = NX * NC
MEMBERS = NY * NZ
CAP = 32
TILES = 4
BLOCK = MEMBERS * TILES
MEET = 4
W = 128
ROWS = 512
HALF = ROWS // 2
CODED = HALF + 16

PEERS = ((1, 0), (3, 0), (1, 1), (3, 1), (2, 0), (2, 1), (0, 1))
OWN, SIBLING, NEAR, FAR = 7, 6, (0, 1, 2, 3), (4, 5)

CASES = tuple((h, w) for h in (0, 1) for w in (0, 1))


def wrap(value, size):
    return lax.rem(value + size, size)


def encode(value):
    blocks = value.reshape(HALF // 16, 16, W)
    most = jnp.max(jnp.abs(blocks), axis=0)
    power = jnp.ceil(jnp.log2(jnp.maximum(most, 1e-30)) - 14.999)
    whole = jnp.round(blocks * jnp.exp2(-power)[None]).astype(jnp.int32)
    return whole.reshape(HALF, W).astype(jnp.int16), power.astype(jnp.int32).astype(jnp.int16)


def decode(ref):
    factor = jnp.exp2(ref[pl.ds(HALF, 16), :].astype(jnp.int32).astype(jnp.float32))
    whole = ref[pl.ds(0, HALF), :].astype(jnp.int32).astype(jnp.float32)
    return (whole.reshape(HALF // 16, 16, W) * factor[None]).reshape(HALF, W)


def write(ref, value):
    whole, power = encode(value)
    ref[pl.ds(0, HALF), :] = whole
    ref[pl.ds(HALF, 16), :] = power


class Reduce:
    def __init__(self, at, along, pair, parts, bufs, sems, out):
        self.at, self.along, self.pair, self.parts, self.out = at, along, pair, parts, out
        self.a_in, self.b_in, self.c_in, self.summed, self.coded, self.d_in, self.e_in, self.f_in = bufs
        self.sems = sems
        self.copies = {}

    def second(self, i, k):
        h, w = CASES[i]
        sense = 1 - 2 * w
        return wrap(self.at[1 - h] + (2, -sense, sense, 0)[k], 4)

    def send(self, name, src, dst, leg, step, *index):
        send_sem, recv_sem = self.sems[name]
        key = index if len(index) > 1 else index[0]
        copy = pltpu.make_async_remote_copy(
            src_ref=src, dst_ref=dst, send_sem=send_sem.at[key], recv_sem=recv_sem.at[key],
            device_id=self.along(leg, step), device_id_type=MESH,
        )
        copy.start()
        self.copies[(name,) + index] = copy

    def start(self):
        for k in range(4):
            for i, (h, w) in enumerate(CASES):
                sense = 1 - 2 * w
                self.send(
                    "a", self.parts.at[h, w, wrap(self.at[h] + 2, 4), self.second(i, k)], self.a_in.at[i, k], h, sense, i, k
                )
        for i, (h, w) in enumerate(CASES):
            sense = 1 - 2 * w
            self.send("b", self.parts.at[h, w, wrap(self.at[h] - sense, 4)], self.b_in.at[i], h, -sense, i)

    def relay(self):
        for k in range(4):
            for i, (h, w) in enumerate(CASES):
                sense = 1 - 2 * w
                self.copies["a", i, k].wait()
                own = self.parts.at[h, w, wrap(self.at[h] + sense, 4), self.second(i, k)]
                write(self.a_in.at[i, k], decode(self.a_in.at[i, k]) + decode(own))
                self.send("c", self.a_in.at[i, k], self.c_in.at[i, k], h, sense, i, k)

    def turn(self):
        for i in range(4):
            self.copies["b", i].wait()
        for k in range(4):
            for i, (h, w) in enumerate(CASES):
                sense = 1 - 2 * w
                q = self.second(i, k)
                self.copies["c", i, k].wait()
                value = decode(self.c_in.at[i, k]) + decode(self.parts.at[h, w, self.at[h], q]) + decode(self.b_in.at[i, q])
                if k == 0:
                    write(self.coded.at[i, 0], value)
                    self.send("d", self.coded.at[i, 0], self.d_in.at[i], 1 - h, sense, i)
                elif k == 1:
                    write(self.coded.at[i, 1], value)
                    self.send("e", self.coded.at[i, 1], self.e_in.at[i], 1 - h, -sense, i)
                else:
                    self.summed[i, k - 2] = value

    def pass_on(self):
        for i, (h, w) in enumerate(CASES):
            sense = 1 - 2 * w
            self.copies["d", i].wait()
            write(self.d_in.at[i], decode(self.d_in.at[i]) + self.summed[i, 0])
            self.send("f", self.d_in.at[i], self.f_in.at[i], 1 - h, sense, i)

    def finish(self):
        for i, (h, w) in enumerate(CASES):
            self.copies["e", i].wait()
            self.copies["f", i].wait()
            self.summed[i, 1] = self.summed[i, 1] + decode(self.e_in.at[i]) + decode(self.f_in.at[i])
            self.copies["out", i] = pltpu.make_async_copy(
                self.summed.at[i, 1], self.out.at[2 * self.pair + w, pl.ds(h * HALF, HALF)], self.sems["out"].at[i]
            )
            self.copies["out", i].start()

    def close(self):
        for i in range(4):
            self.copies["out", i].wait()


REDUCE_SEMS = (("a", (4, 4)), ("b", (4,)), ("c", (4, 4)), ("d", (4,)), ("e", (4,)), ("f", (4,)))


def reduce_scratch():
    tile = (CODED, W)
    shapes = [
        pltpu.VMEM((2, 2, 4, 4) + tile, jnp.int16),
        pltpu.VMEM((4, 4) + tile, jnp.int16),
        pltpu.VMEM((4, 4) + tile, jnp.int16),
        pltpu.VMEM((4, 4) + tile, jnp.int16),
        pltpu.VMEM((4, 2, HALF, W), jnp.float32),
        pltpu.VMEM((4, 2) + tile, jnp.int16),
        pltpu.VMEM((4,) + tile, jnp.int16),
        pltpu.VMEM((4,) + tile, jnp.int16),
        pltpu.VMEM((4,) + tile, jnp.int16),
    ]
    for _, shape in REDUCE_SEMS:
        shapes += [pltpu.SemaphoreType.DMA(shape)] * 2
    return shapes + [pltpu.SemaphoreType.DMA((4,))]


def ladder_kernel(order, labels, integrals, amps, out, *scratch):
    scratch = list(scratch)

    def take(n):
        taken = scratch[:n]
        del scratch[:n]
        return taken

    stored, outgoing, block_amps, label_in, label_s, total = take(6)
    arrived = take(8)
    tile_send, tile_recv, label_send, label_recv, amp_send, amp_recv, local_sem, smem_sem = take(8)

    group = lax.axis_index("group")
    member = lax.axis_index("member")
    x, core, y, z = group // NC, lax.rem(group, NC), member // NZ, lax.rem(member, NZ)

    def across(k):
        dx, dc = PEERS[k]
        return (wrap(x + dx, NX) * NC + wrap(core + dc, NC), member)

    def along(axis, step):
        if axis == 0:
            return (group, wrap(y + step, NY) * NZ + z)
        return (group, y * NZ + wrap(z + step, NZ))

    sums = []
    for pair in (0, 1):
        parts, *bufs = take(9)
        sems = {name: tuple(take(2)) for name, _ in REDUCE_SEMS}
        (sems["out"],) = take(1)
        sums.append(Reduce((y, z), along, pair, parts, bufs, sems, out))

    load = pltpu.make_async_copy(integrals, stored, local_sem.at[0])
    load.start()
    own_amps = pltpu.make_async_copy(amps, block_amps.at[member], local_sem.at[1])
    own_amps.start()
    own_label = pltpu.make_async_copy(labels.at[group], label_in.at[OWN], local_sem.at[2])
    own_label.start()

    barrier = pltpu.get_barrier_semaphore()
    for k in range(7):
        pl.semaphore_signal(barrier, inc=1, device_id=across(k), device_id_type=MESH)
    for axis in (0, 1):
        for step in (1, 2, 3):
            pl.semaphore_signal(barrier, inc=1, device_id=along(axis, step), device_id_type=MESH)
    pl.semaphore_wait(barrier, 13)

    def send(src, dst, send_sem, recv_sem, target):
        copy = pltpu.make_async_remote_copy(
            src_ref=src, dst_ref=dst, send_sem=send_sem, recv_sem=recv_sem, device_id=target, device_id_type=MESH
        )
        copy.start()
        return copy

    first, others = {}, []
    count = 0
    for axis in (0, 1):
        half = pl.ds(axis * 2, 2)
        for step in (1, 3, 2):
            first[axis, step] = send(
                amps.at[half], block_amps.at[member, half], amp_send.at[count], amp_recv.at[count], along(axis, step)
            )
            count += 1

    load.wait()
    tile_copies, label_copies = [], []
    for k in range(7):
        target = across(k)

        @pl.loop(0, CAP)
        def _(t):
            outgoing[k, t] = stored[order[target[0] * CAP + t]]

        tile_copies.append(send(outgoing.at[k], arrived[k], tile_send.at[k], tile_recv.at[k], target))
        label_copies.append(send(labels.at[target[0]], label_in.at[k], label_send.at[k], label_recv.at[k], target))

    @pl.loop(0, CAP)
    def _(t):
        arrived[OWN][t] = stored[order[group * CAP + t]]

    for came in (0, 1, 3, 2):
        for axis in (0, 1):
            half = pl.ds(axis * 2, 2)
            if came == 0:
                where, source = member, amps.at[half]
            else:
                first[axis, came].wait_recv()
                back = 4 - came
                where = wrap(y + back, NY) * NZ + z if axis == 0 else y * NZ + wrap(z + back, NZ)
                source = block_amps.at[where, half]
            for step in (1, 3, 2):
                others.append(
                    send(source, block_amps.at[where, half], amp_send.at[count], amp_recv.at[count], along(1 - axis, step))
                )
                count += 1

    for k in range(8):
        if k == OWN:
            own_label.wait()
        else:
            label_copies[k].wait()
        move = pltpu.make_async_copy(label_in.at[k], label_s.at[k], smem_sem.at[k])
        move.start()
        move.wait()
    own_amps.wait()
    for copy in first.values():
        copy.wait_send()
    for copy in others:
        copy.wait()

    def contract(pair, sources, opening):
        @pl.loop(0, MEMBERS)
        def _(d):
            left, right = [], []
            for k in sources:
                for j in range(MEET):
                    entry = label_s[k, 0, pair * 64 + d * MEET + j]
                    tile = arrived[k][entry & 31]
                    source = lax.shift_right_logical(entry, 8) & 63
                    column = lax.shift_right_logical(entry, 16)
                    left.append(block_amps[source // TILES, source & 3])
                    none = jnp.zeros_like(tile)
                    right.append(
                        jnp.concatenate([jnp.where(column == 0, tile, none), jnp.where(column == 1, tile, none)], axis=1)
                    )
            product = jnp.dot(
                jnp.concatenate(left, axis=1), jnp.concatenate(right, axis=0), preferred_element_type=jnp.float32
            )
            if opening:
                total[d] = product
            else:
                total[d] += product

    def code(pair):
        @pl.loop(0, MEMBERS)
        def _(d):
            one, two = d // NZ, lax.rem(d, NZ)
            for h, w in CASES:
                p, q = (one, two) if h == 0 else (two, one)
                write(sums[pair].parts.at[h, w, p, q], total[d, pl.ds(h * HALF, HALF), pl.ds(w * W, W)])

    tile_copies[SIBLING].wait()
    contract(0, (OWN, SIBLING), True)
    for k in NEAR:
        tile_copies[k].wait()
    contract(0, NEAR, False)
    for k in FAR:
        tile_copies[k].wait()
    contract(0, FAR, False)
    code(0)
    sums[0].start()
    contract(1, (OWN, SIBLING), True)
    sums[0].relay()
    contract(1, NEAR, False)
    sums[0].turn()
    contract(1, FAR, False)
    code(1)
    sums[1].start()
    sums[0].pass_on()
    sums[0].finish()
    sums[1].relay()
    sums[1].turn()
    sums[1].pass_on()
    sums[1].finish()
    sums[0].close()
    sums[1].close()


def ladder(order, labels, integrals, amps):
    dma = pltpu.SemaphoreType.DMA
    return pl.pallas_call(
        ladder_kernel,
        out_shape=jax.ShapeDtypeStruct((TILES, ROWS, W), jnp.float32),
        in_specs=[SMEM, ANY, ANY, ANY],
        out_specs=ANY,
        scratch_shapes=[
            pltpu.VMEM(integrals.shape, jnp.bfloat16),
            pltpu.VMEM((7, CAP, W, W), jnp.bfloat16),
            pltpu.VMEM((MEMBERS, TILES, ROWS, W), jnp.bfloat16),
            pltpu.VMEM((GROUPS, 8, 128), jnp.int32),
            pltpu.SMEM((GROUPS, 8, 128), jnp.int32),
            pltpu.VMEM((MEMBERS, ROWS, 2 * W), jnp.float32),
        ]
        + [pltpu.VMEM((CAP, W, W), jnp.bfloat16)] * 8
        + [dma((7,)), dma((7,)), dma((7,)), dma((7,)), dma((30,)), dma((30,)), dma((3,)), dma((8,))]
        + reduce_scratch() * 2,
        compiler_params=pltpu.CompilerParams(collective_id=0, has_side_effects=True, vmem_limit_bytes=60 << 20),
        name="ladder",
    )(order, labels, integrals, amps)


def slots(plan):
    rows = plan.shape[0]
    group = plan[:, 2] // MEMBERS
    source = plan[:, 0] % BLOCK
    target = plan[:, 1] % BLOCK
    tile = target % TILES
    row = jnp.arange(rows, dtype=jnp.int32)
    before = row[None, :] < row[:, None]
    here = group[None, :] == group[:, None]
    slot = jnp.sum((here & before).astype(jnp.int32), axis=1)
    meet = group * 128 + (tile // 2) * 64 + (target // TILES) * MEET
    place = meet + jnp.sum(((meet[None, :] == meet[:, None]) & before).astype(jnp.int32), axis=1)
    entry = slot + 256 * source + 65536 * (tile % 2)
    at = jnp.arange(GROUPS * CAP, dtype=jnp.int32)[:, None] == (group * CAP + slot)[None, :]
    order = jnp.sum(jnp.where(at, row[None, :], 0), axis=1)
    at = jnp.arange(GROUPS * 128, dtype=jnp.int32)[:, None] == place[None, :]
    labels = 2 * 65536 + jnp.sum(jnp.where(at, entry[None, :] - 2 * 65536, 0), axis=1)
    return order, jnp.pad(labels.reshape(GROUPS, 1, 128), ((0, 0), (0, 7), (0, 0)))


def on_device(amplitudes, integrals, task_plan):
    order, labels = slots(task_plan)
    return ladder(order, labels, integrals, amplitudes)


def solution(mesh):
    in_specs = (
        P(("group", "member"), None, None),
        P(("group", "member"), None, None),
        P(("group", "member"), None),
    )
    out_specs = P(("group", "member"), None, None)
    return jax.shard_map(
        on_device, mesh=mesh, in_specs=in_specs, out_specs=out_specs, check_vma=False
    )
```

```python
import jax
import jax.numpy as jnp
from jax import lax
from jax.experimental import pallas as pl
from jax.experimental.pallas import tpu as pltpu
from jax.sharding import PartitionSpec as P

MESH = pl.DeviceIdType.MESH
ANY = pl.BlockSpec(memory_space=pl.ANY)
VMEM = pl.BlockSpec(memory_space=pltpu.VMEM)
SMEM = pl.BlockSpec(memory_space=pltpu.SMEM)

NX, NC, NY, NZ = 4, 2, 4, 4
GROUPS = NX * NC
MEMBERS = NY * NZ
CAP = 32
TILES = 4
BLOCK = MEMBERS * TILES
MEET = 4
W = 128
ROWS = 512
HALF = ROWS // 2
CODED = HALF + 16

PEERS = ((1, 0), (3, 0), (1, 1), (3, 1), (0, 1), (2, 0), (2, 1))
NEAR, SIBLING, FAR, OWN = (0, 1, 2, 3), 4, (5, 6), 7
FIRST = NEAR + (SIBLING,)

CASES = tuple((h, w) for h in (0, 1) for w in (0, 1))


def wrap(value, size):
    return lax.rem(value + size, size)


def encode(value):
    blocks = value.reshape(HALF // 16, 16, W)
    most = jnp.max(jnp.abs(blocks), axis=0)
    power = jnp.ceil(jnp.log2(jnp.maximum(most, 1e-30)) - 14.999)
    whole = jnp.round(blocks * jnp.exp2(-power)[None]).astype(jnp.int32)
    return whole.reshape(HALF, W).astype(jnp.int16), power.astype(jnp.int32).astype(jnp.int16)


def decode(ref):
    factor = jnp.exp2(ref[pl.ds(HALF, 16), :].astype(jnp.int32).astype(jnp.float32))
    whole = ref[pl.ds(0, HALF), :].astype(jnp.int32).astype(jnp.float32)
    return (whole.reshape(HALF // 16, 16, W) * factor[None]).reshape(HALF, W)


def write(ref, value):
    whole, power = encode(value)
    ref[pl.ds(0, HALF), :] = whole
    ref[pl.ds(HALF, 16), :] = power


class Reduce:
    def __init__(self, at, along, pair, total, parts, bufs, sems, out):
        self.at, self.along, self.pair, self.total, self.parts, self.out = at, along, pair, total, parts, out
        self.a_in, self.b_in, self.c_in, self.d_in, self.e_in, self.f_in = bufs
        self.sems = sems
        self.copies = {}

    def second(self, i, k):
        h, w = CASES[i]
        sense = 1 - 2 * w
        return wrap(self.at[1 - h] + (2, -sense, sense, 0)[k], 4)

    def send(self, name, src, dst, leg, step, *index):
        send_sem, recv_sem = self.sems[name]
        key = index if len(index) > 1 else index[0]
        copy = pltpu.make_async_remote_copy(
            src_ref=src, dst_ref=dst, send_sem=send_sem.at[key], recv_sem=recv_sem.at[key],
            device_id=self.along(leg, step), device_id_type=MESH,
        )
        copy.start()
        self.copies[(name,) + index] = copy

    def own(self, i, q):
        h, w = CASES[i]
        d = self.at[0] * NZ + q if h == 0 else q * NZ + self.at[1]
        return self.total.at[d, pl.ds(h * HALF, HALF), pl.ds(w * W, W)]

    def code(self):
        @pl.loop(0, 12)
        def _(t):
            r, q = t // 4, lax.rem(t, 4)
            for h, w in CASES:
                p = wrap(self.at[h] + r + 1, 4)
                d = p * NZ + q if h == 0 else q * NZ + p
                write(self.parts.at[h, w, r, q], self.total[d, pl.ds(h * HALF, HALF), pl.ds(w * W, W)])

    def start_far(self):
        for k in range(4):
            for i, (h, w) in enumerate(CASES):
                sense = 1 - 2 * w
                self.send(
                    "a", self.parts.at[h, w, 1, self.second(i, k)], self.a_in.at[i, k], h, sense, i, k
                )

    def start_near(self):
        for i, (h, w) in enumerate(CASES):
            sense = 1 - 2 * w
            self.send("b", self.parts.at[h, w, 1 + sense], self.b_in.at[i], h, -sense, i)

    def relay(self):
        for k in range(4):
            for i, (h, w) in enumerate(CASES):
                sense = 1 - 2 * w
                self.copies["a", i, k].wait()
                own = self.parts.at[h, w, 1 - sense, self.second(i, k)]
                write(self.a_in.at[i, k], decode(self.a_in.at[i, k]) + decode(own))
                self.send("c", self.a_in.at[i, k], self.c_in.at[i, k], h, sense, i, k)

    def turn(self):
        for i in range(4):
            self.copies["b", i].wait()
        for k in range(4):
            for i, (h, w) in enumerate(CASES):
                sense = 1 - 2 * w
                q = self.second(i, k)
                self.copies["c", i, k].wait()
                value = decode(self.c_in.at[i, k]) + self.own(i, q)[...] + decode(self.b_in.at[i, q])
                if k == 0:
                    write(self.a_in.at[i, 0], value)
                    self.send("d", self.a_in.at[i, 0], self.d_in.at[i], 1 - h, sense, i)
                elif k == 1:
                    write(self.a_in.at[i, 1], value)
                    self.send("e", self.a_in.at[i, 1], self.e_in.at[i], 1 - h, -sense, i)
                else:
                    self.own(i, q)[...] = value

    def pass_on(self):
        for i, (h, w) in enumerate(CASES):
            sense = 1 - 2 * w
            self.copies["d", i].wait()
            write(self.d_in.at[i], decode(self.d_in.at[i]) + self.own(i, self.second(i, 2))[...])
            self.send("f", self.d_in.at[i], self.f_in.at[i], 1 - h, sense, i)

    def finish(self):
        for i, (h, w) in enumerate(CASES):
            self.copies["e", i].wait()
            self.copies["f", i].wait()
            own = self.own(i, self.second(i, 3))
            own[...] = own[...] + decode(self.e_in.at[i]) + decode(self.f_in.at[i])
            self.copies["out", i] = pltpu.make_async_copy(
                own, self.out.at[2 * self.pair + w, pl.ds(h * HALF, HALF)], self.sems["out"].at[i]
            )
            self.copies["out", i].start()

    def close(self):
        for i in range(4):
            self.copies["out", i].wait()


REDUCE_SEMS = (("a", (4, 4)), ("b", (4,)), ("c", (4, 4)), ("d", (4,)), ("e", (4,)), ("f", (4,)))


def reduce_scratch():
    tile = (CODED, W)
    shapes = [
        pltpu.VMEM((2, 2, 3, 4) + tile, jnp.int16),
        pltpu.VMEM((4, 4) + tile, jnp.int16),
        pltpu.VMEM((4, 4) + tile, jnp.int16),
        pltpu.VMEM((4, 4) + tile, jnp.int16),
        pltpu.VMEM((4,) + tile, jnp.int16),
        pltpu.VMEM((4,) + tile, jnp.int16),
        pltpu.VMEM((4,) + tile, jnp.int16),
    ]
    for _, shape in REDUCE_SEMS:
        shapes += [pltpu.SemaphoreType.DMA(shape)] * 2
    return shapes + [pltpu.SemaphoreType.DMA((4,))]


def ladder_kernel(order, labels, integrals, amps, out, *scratch):
    scratch = list(scratch)

    def take(n):
        taken = scratch[:n]
        del scratch[:n]
        return taken

    stored, outgoing, block_amps, label_in, label_s, *totals = take(7)
    arrived = take(7) + [stored]
    tile_send, tile_recv, label_send, label_recv, amp_send, amp_recv, local_sem, smem_sem = take(8)

    group = lax.axis_index("group")
    member = lax.axis_index("member")
    x, core, y, z = group // NC, lax.rem(group, NC), member // NZ, lax.rem(member, NZ)

    def across(k):
        dx, dc = PEERS[k]
        return (wrap(x + dx, NX) * NC + wrap(core + dc, NC), member)

    def along(axis, step):
        if axis == 0:
            return (group, wrap(y + step, NY) * NZ + z)
        return (group, y * NZ + wrap(z + step, NZ))

    sums = []
    for pair in (0, 1):
        parts, *bufs = take(7)
        sems = {name: tuple(take(2)) for name, _ in REDUCE_SEMS}
        (sems["out"],) = take(1)
        sums.append(Reduce((y, z), along, pair, totals[pair], parts, bufs, sems, out))

    load = pltpu.make_async_copy(integrals, stored, local_sem.at[0])
    load.start()
    own_amps = pltpu.make_async_copy(amps, block_amps.at[member], local_sem.at[1])
    own_amps.start()
    own_label = pltpu.make_async_copy(labels.at[group], label_in.at[OWN], local_sem.at[2])
    own_label.start()

    barrier = pltpu.get_barrier_semaphore()
    for k in range(7):
        pl.semaphore_signal(barrier, inc=1, device_id=across(k), device_id_type=MESH)
    for axis in (0, 1):
        for step in (1, -1):
            pl.semaphore_signal(barrier, inc=1, device_id=along(axis, step), device_id_type=MESH)
    pl.semaphore_wait(barrier, 11)

    def send(src, dst, send_sem, recv_sem, target):
        copy = pltpu.make_async_remote_copy(
            src_ref=src, dst_ref=dst, send_sem=send_sem, recv_sem=recv_sem, device_id=target, device_id_type=MESH
        )
        copy.start()
        return copy

    sent = []

    def pass_amps(where, tiles, axis, step):
        count = len(sent)
        ref = block_amps.at[where, pl.ds(tiles[0], len(tiles))]
        source = amps.at[pl.ds(tiles[0], len(tiles))] if where is member else ref
        copy = send(source, ref, amp_send.at[count], amp_recv.at[count], along(axis, step))
        sent.append(copy)
        return copy

    def moved(axis, place, step):
        a, b = place
        return (wrap(a + step, 4), b) if axis == 0 else (a, wrap(b + step, 4))

    def index(place):
        return place[0] * NZ + place[1]

    here = (y, z)
    leg_one = {}
    for h in (0, 1):
        for step in (1, -1):
            leg_one[h, step] = pass_amps(member, (2 * h, 2 * h + 1), h, step)

    load.wait()
    tile_copies, label_copies = {}, {}

    def post(k, slot):
        target = across(k)

        @pl.loop(0, CAP)
        def _(t):
            outgoing[slot, t] = stored[order[target[0] * CAP + t]]

        tile_copies[k] = send(outgoing.at[slot], arrived[k], tile_send.at[k], tile_recv.at[k], target)

    for k in FIRST:
        post(k, k)
    for k in range(7):
        target = across(k)
        label_copies[k] = send(labels.at[target[0]], label_in.at[k], label_send.at[k], label_recv.at[k], target)

    leg_two, leg_one_on = {}, {}

    def second_leg(h, b):
        where = member if b == 0 else index(moved(h, here, -b))
        for step in (1, -1):
            leg_two[h, b, step] = pass_amps(where, (2 * h, 2 * h + 1), 1 - h, step)

    for h in (0, 1):
        second_leg(h, 0)
    for h in (0, 1):
        for step in (1, -1):
            leg_one[h, step].wait_recv()
            tile = 2 * h + (step == -1)
            leg_one_on[h, step] = pass_amps(index(moved(h, here, -step)), (tile,), h, step)
            second_leg(h, step)
    leg_two_on = []

    def second_leg_on(h, b):
        for step in (1, -1):
            leg_two[h, b, step].wait_recv()
            tile = 2 * h + (step == -1)
            place = moved(1 - h, moved(h, here, -b), -step)
            leg_two_on.append(pass_amps(index(place), (tile,), 1 - h, step))

    for h in (0, 1):
        second_leg_on(h, 0)
    for h in (0, 1):
        for step in (1, -1):
            leg_one_on[h, step].wait_recv()
        second_leg(h, 2)
    tile_copies[SIBLING].wait_send()
    post(FAR[0], SIBLING)
    for b in (1, -1, 2):
        for h in (0, 1):
            second_leg_on(h, b)
    for k in NEAR:
        tile_copies[k].wait_send()

    own_label.wait()
    for k in range(7):
        label_copies[k].wait()
    move = pltpu.make_async_copy(label_in, label_s, smem_sem)
    move.start()
    move.wait()
    own_amps.wait()
    for copy in leg_two_on:
        copy.wait_recv()
    for copy in sent:
        copy.wait_send()

    def contract(pairs, sources, opening, unroll=1):
        @pl.loop(0, MEMBERS // unroll)
        def _(turn):
            for d in [turn * unroll + u for u in range(unroll)]:
                for pair in pairs:
                    left, right = [], []
                    for k in sources:
                        for j in range(MEET):
                            entry = label_s[k, 0, pair * 64 + d * MEET + j]
                            row = entry & 255
                            tile = arrived[k][jnp.minimum(row, integrals.shape[0] - 1 if k == OWN else CAP - 1)]
                            source = lax.shift_right_logical(entry, 8) & 63
                            column = lax.shift_right_logical(entry, 16)
                            left.append(block_amps[source // TILES, source & 3])
                            none = jnp.zeros_like(tile)
                            right.append(
                                jnp.concatenate([jnp.where(column == 0, tile, none), jnp.where(column == 1, tile, none)], axis=1)
                            )
                    product = jnp.dot(
                        jnp.concatenate(left, axis=1), jnp.concatenate(right, axis=0), preferred_element_type=jnp.float32
                    )
                    if opening:
                        totals[pair][d] = product
                    else:
                        totals[pair][d] += product

    tile_copies[SIBLING].wait_recv()
    post(FAR[1], NEAR[0])
    contract((0, 1), (OWN, SIBLING), True)
    for k in NEAR:
        tile_copies[k].wait_recv()
    contract((0, 1), NEAR, False)
    tile_copies[FAR[0]].wait()
    contract((0, 1), FAR[:1], False, 2)
    tile_copies[FAR[1]].wait()
    contract((0,), FAR[1:], False, 4)
    sums[0].code()
    sums[0].start_far()
    contract((1,), FAR[1:], False, 4)
    sums[1].code()
    sums[0].start_near()
    sums[1].start_far()
    sums[0].relay()
    sums[1].start_near()
    sums[1].relay()
    sums[0].turn()
    sums[1].turn()
    sums[0].pass_on()
    sums[1].pass_on()
    sums[0].finish()
    sums[1].finish()
    sums[0].close()
    sums[1].close()


def ladder(order, labels, integrals, amps):
    dma = pltpu.SemaphoreType.DMA
    return pl.pallas_call(
        ladder_kernel,
        out_shape=jax.ShapeDtypeStruct((TILES, ROWS, W), jnp.float32),
        in_specs=[SMEM, ANY, ANY, ANY],
        out_specs=ANY,
        scratch_shapes=[
            pltpu.VMEM(integrals.shape, jnp.bfloat16),
            pltpu.VMEM((len(FIRST), CAP, W, W), jnp.bfloat16),
            pltpu.VMEM((MEMBERS, TILES, ROWS, W), jnp.bfloat16),
            pltpu.VMEM((GROUPS, 8, 128), jnp.int32),
            pltpu.SMEM((GROUPS, 8, 128), jnp.int32),
            pltpu.VMEM((MEMBERS, ROWS, 2 * W), jnp.float32),
            pltpu.VMEM((MEMBERS, ROWS, 2 * W), jnp.float32),
        ]
        + [pltpu.VMEM((CAP, W, W), jnp.bfloat16)] * 7
        + [dma((7,)), dma((7,)), dma((7,)), dma((7,)), dma((40,)), dma((40,)), dma((3,)), dma]
        + reduce_scratch() * 2,
        compiler_params=pltpu.CompilerParams(collective_id=0, has_side_effects=True, vmem_limit_bytes=60 << 20),
        name="ladder",
    )(order, labels, integrals, amps)


def slots(plan):
    rows = plan.shape[0]
    group = plan[:, 2] // MEMBERS
    source = plan[:, 0] % BLOCK
    target = plan[:, 1] % BLOCK
    tile = target % TILES
    row = jnp.arange(rows, dtype=jnp.int32)
    before = row[None, :] < row[:, None]
    here = group[None, :] == group[:, None]
    slot = jnp.sum((here & before).astype(jnp.int32), axis=1)
    meet = group * 128 + (tile // 2) * 64 + (target // TILES) * MEET
    place = meet + jnp.sum(((meet[None, :] == meet[:, None]) & before).astype(jnp.int32), axis=1)
    stay = group == lax.axis_index("group")
    entry = jnp.where(stay, row, slot) + 256 * source + 65536 * (tile % 2)
    at = jnp.arange(GROUPS * CAP, dtype=jnp.int32)[:, None] == (group * CAP + slot)[None, :]
    order = jnp.sum(jnp.where(at, row[None, :], 0), axis=1)
    at = jnp.arange(GROUPS * 128, dtype=jnp.int32)[:, None] == place[None, :]
    labels = 2 * 65536 + jnp.sum(jnp.where(at, entry[None, :] - 2 * 65536, 0), axis=1)
    return order, jnp.pad(labels.reshape(GROUPS, 1, 128), ((0, 0), (0, 7), (0, 0)))


def on_device(amplitudes, integrals, task_plan):
    order, labels = slots(task_plan)
    return ladder(order, labels, integrals, amplitudes)


def solution(mesh):
    in_specs = (
        P(("group", "member"), None, None),
        P(("group", "member"), None, None),
        P(("group", "member"), None),
    )
    out_specs = P(("group", "member"), None, None)
    return jax.shard_map(
        on_device, mesh=mesh, in_specs=in_specs, out_specs=out_specs, check_vma=False
    )
```

```python
import functools

import jax
import jax.numpy as jnp
from jax import lax
from jax.experimental import pallas as pl
from jax.experimental.pallas import tpu as pltpu
from jax.sharding import PartitionSpec as P

MESH = pl.DeviceIdType.MESH
ANY = pl.BlockSpec(memory_space=pl.ANY)
VMEM = pl.BlockSpec(memory_space=pltpu.VMEM)
SMEM = pl.BlockSpec(memory_space=pltpu.SMEM)

NX, NC, NY, NZ = 4, 2, 4, 4
GROUPS = NX * NC
MEMBERS = NY * NZ
CAP = 32
TILES = 4
BLOCK = MEMBERS * TILES
MEET = 4
EARLY = 26
W = 128
ROWS = 512
HALF = ROWS // 2
CODED = HALF + 16

PEERS = ((1, 0), (3, 0), (1, 1), (3, 1), (0, 1), (2, 0), (2, 1))
NEAR, SIBLING, FAR, OWN = (0, 1, 2, 3), 4, (5, 6), 7
FIRST = NEAR + (SIBLING,)

CASES = tuple((h, w) for h in (0, 1) for w in (0, 1))


def wrap(value, size):
    return lax.rem(value + size, size)


def encode(value):
    blocks = value.reshape(HALF // 16, 16, W)
    most = jnp.max(jnp.abs(blocks), axis=0)
    power = jnp.ceil(jnp.log2(jnp.maximum(most, 1e-30)) - 14.999)
    whole = jnp.round(blocks * jnp.exp2(-power)[None]).astype(jnp.int32)
    return whole.reshape(HALF, W).astype(jnp.int16), power.astype(jnp.int32).astype(jnp.int16)


def decode(ref):
    factor = jnp.exp2(ref[pl.ds(HALF, 16), :].astype(jnp.int32).astype(jnp.float32))
    whole = ref[pl.ds(0, HALF), :].astype(jnp.int32).astype(jnp.float32)
    return (whole.reshape(HALF // 16, 16, W) * factor[None]).reshape(HALF, W)


def write(ref, value):
    whole, power = encode(value)
    ref[pl.ds(0, HALF), :] = whole
    ref[pl.ds(HALF, 16), :] = power


class Reduce:
    def __init__(self, at, along, pair, total, parts, bufs, sems, out):
        self.at, self.along, self.pair, self.total, self.parts, self.out = at, along, pair, total, parts, out
        self.a_in, self.b_in, self.c_in, self.d_in, self.e_in, self.f_in = bufs
        self.sems = sems
        self.copies = {}

    def second(self, i, k):
        h, w = CASES[i]
        sense = 1 - 2 * w
        return wrap(self.at[1 - h] + (2, -sense, sense, 0)[k], 4)

    def send(self, name, src, dst, leg, step, *index):
        send_sem, recv_sem = self.sems[name]
        key = index if len(index) > 1 else index[0]
        copy = pltpu.make_async_remote_copy(
            src_ref=src, dst_ref=dst, send_sem=send_sem.at[key], recv_sem=recv_sem.at[key],
            device_id=self.along(leg, step), device_id_type=MESH,
        )
        copy.start()
        self.copies[(name,) + index] = copy

    def own(self, i, q):
        h, w = CASES[i]
        d = self.at[0] * NZ + q if h == 0 else q * NZ + self.at[1]
        return self.total.at[d, pl.ds(h * HALF, HALF), pl.ds(w * W, W)]

    def code(self):
        @pl.loop(0, 12)
        def _(t):
            r, q = t // 4, lax.rem(t, 4)
            for h, w in CASES:
                p = wrap(self.at[h] + r + 1, 4)
                d = p * NZ + q if h == 0 else q * NZ + p
                write(self.parts.at[h, w, r, q], self.total[d, pl.ds(h * HALF, HALF), pl.ds(w * W, W)])

    def start_far(self):
        for k in range(4):
            for i, (h, w) in enumerate(CASES):
                sense = 1 - 2 * w
                self.send(
                    "a", self.parts.at[h, w, 1, self.second(i, k)], self.a_in.at[i, k], h, sense, i, k
                )

    def start_near(self):
        for i, (h, w) in enumerate(CASES):
            sense = 1 - 2 * w
            self.send("b", self.parts.at[h, w, 1 + sense], self.b_in.at[i], h, -sense, i)

    def relay(self):
        for k in range(4):
            for i, (h, w) in enumerate(CASES):
                sense = 1 - 2 * w
                self.copies["a", i, k].wait()
                own = self.parts.at[h, w, 1 - sense, self.second(i, k)]
                write(self.a_in.at[i, k], decode(self.a_in.at[i, k]) + decode(own))
                self.send("c", self.a_in.at[i, k], self.c_in.at[i, k], h, sense, i, k)

    def turn(self):
        for i in range(4):
            self.copies["b", i].wait()
        for k in range(4):
            for i, (h, w) in enumerate(CASES):
                sense = 1 - 2 * w
                q = self.second(i, k)
                self.copies["c", i, k].wait()
                value = decode(self.c_in.at[i, k]) + self.own(i, q)[...] + decode(self.b_in.at[i, q])
                if k == 0:
                    write(self.a_in.at[i, 0], value)
                    self.send("d", self.a_in.at[i, 0], self.d_in.at[i], 1 - h, sense, i)
                elif k == 1:
                    write(self.a_in.at[i, 1], value)
                    self.send("e", self.a_in.at[i, 1], self.e_in.at[i], 1 - h, -sense, i)
                else:
                    self.own(i, q)[...] = value

    def pass_on(self):
        for i, (h, w) in enumerate(CASES):
            sense = 1 - 2 * w
            self.copies["d", i].wait()
            write(self.d_in.at[i], decode(self.d_in.at[i]) + self.own(i, self.second(i, 2))[...])
            self.send("f", self.d_in.at[i], self.f_in.at[i], 1 - h, sense, i)

    def finish(self):
        for i, (h, w) in enumerate(CASES):
            self.copies["e", i].wait()
            self.copies["f", i].wait()
            own = self.own(i, self.second(i, 3))
            own[...] = own[...] + decode(self.e_in.at[i]) + decode(self.f_in.at[i])
            self.copies["out", i] = pltpu.make_async_copy(
                own, self.out.at[2 * self.pair + w, pl.ds(h * HALF, HALF)], self.sems["out"].at[i]
            )
            self.copies["out", i].start()

    def close(self):
        for i in range(4):
            self.copies["out", i].wait()


REDUCE_SEMS = (("a", (4, 4)), ("b", (4,)), ("c", (4, 4)), ("d", (4,)), ("e", (4,)), ("f", (4,)))


def reduce_scratch():
    tile = (CODED, W)
    shapes = [
        pltpu.VMEM((2, 2, 3, 4) + tile, jnp.int16),
        pltpu.VMEM((4, 4) + tile, jnp.int16),
        pltpu.VMEM((4, 4) + tile, jnp.int16),
        pltpu.VMEM((4, 4) + tile, jnp.int16),
        pltpu.VMEM((4,) + tile, jnp.int16),
        pltpu.VMEM((4,) + tile, jnp.int16),
        pltpu.VMEM((4,) + tile, jnp.int16),
    ]
    for _, shape in REDUCE_SEMS:
        shapes += [pltpu.SemaphoreType.DMA(shape)] * 2
    return shapes + [pltpu.SemaphoreType.DMA((4,))]


def ladder_kernel(early, order, labels, integrals, amps, out, excess, *scratch):
    scratch = list(scratch)
    late = CAP - early

    def take(n):
        taken = scratch[:n]
        del scratch[:n]
        return taken

    stored, outgoing, block_amps, label_in, label_s, *totals = take(7)
    arrived = take(7) + [stored]
    if late:
        outgoing_late, *arrived_late = take(8)
    found, found_send, found_recv = take(3)
    tile_send, tile_recv, late_send, late_recv, label_send, label_recv, amp_send, amp_recv, local_sem, smem_sem = take(10)

    group = lax.axis_index("group")
    member = lax.axis_index("member")
    x, core, y, z = group // NC, lax.rem(group, NC), member // NZ, lax.rem(member, NZ)

    def across(k):
        dx, dc = PEERS[k]
        return (wrap(x + dx, NX) * NC + wrap(core + dc, NC), member)

    def along(axis, step):
        if axis == 0:
            return (group, wrap(y + step, NY) * NZ + z)
        return (group, y * NZ + wrap(z + step, NZ))

    sums = []
    for pair in (0, 1):
        parts, *bufs = take(7)
        sems = {name: tuple(take(2)) for name, _ in REDUCE_SEMS}
        (sems["out"],) = take(1)
        sums.append(Reduce((y, z), along, pair, totals[pair], parts, bufs, sems, out))

    load = pltpu.make_async_copy(integrals, stored, local_sem.at[0])
    load.start()
    own_amps = pltpu.make_async_copy(amps, block_amps.at[member], local_sem.at[1])
    own_amps.start()
    own_label = pltpu.make_async_copy(labels.at[group], label_in.at[OWN], local_sem.at[2])
    own_label.start()

    barrier = pltpu.get_barrier_semaphore()
    for k in range(7):
        pl.semaphore_signal(barrier, inc=1, device_id=across(k), device_id_type=MESH)
    for axis in (0, 1):
        for step in (1, -1):
            pl.semaphore_signal(barrier, inc=1, device_id=along(axis, step), device_id_type=MESH)
    pl.semaphore_wait(barrier, 11)

    def send(src, dst, send_sem, recv_sem, target):
        copy = pltpu.make_async_remote_copy(
            src_ref=src, dst_ref=dst, send_sem=send_sem, recv_sem=recv_sem, device_id=target, device_id_type=MESH
        )
        copy.start()
        return copy

    sent = []

    def pass_amps(where, tiles, axis, step):
        count = len(sent)
        ref = block_amps.at[where, pl.ds(tiles[0], len(tiles))]
        source = amps.at[pl.ds(tiles[0], len(tiles))] if where is member else ref
        copy = send(source, ref, amp_send.at[count], amp_recv.at[count], along(axis, step))
        sent.append(copy)
        return copy

    def moved(axis, place, step):
        a, b = place
        return (wrap(a + step, 4), b) if axis == 0 else (a, wrap(b + step, 4))

    def index(place):
        return place[0] * NZ + place[1]

    here = (y, z)
    leg_one = {}
    for h in (0, 1):
        for step in (1, -1):
            leg_one[h, step] = pass_amps(member, (2 * h, 2 * h + 1), h, step)

    leg_two, leg_one_on = {}, {}

    def second_leg(h, b):
        where = member if b == 0 else index(moved(h, here, -b))
        for step in (1, -1):
            leg_two[h, b, step] = pass_amps(where, (2 * h, 2 * h + 1), 1 - h, step)

    for h in (0, 1):
        second_leg(h, 0)

    load.wait()
    tile_copies, label_copies = {}, {}

    def post(k, slot):
        target = across(k)

        @pl.loop(0, early)
        def _(t):
            outgoing[slot, t] = stored[order[target[0] * CAP + t]]

        tile_copies[k] = send(outgoing.at[slot], arrived[k], tile_send.at[k], tile_recv.at[k], target)

    late_copies = {}

    def post_late(k):
        if late:
            late_copies[k] = send(
                outgoing_late.at[k], arrived_late[k], late_send.at[k], late_recv.at[k], across(k)
            )

    def await_late(k):
        if late:
            late_copies[k].wait()

    for k in FIRST:
        post(k, k)
    for k in range(7):
        target = across(k)
        label_copies[k] = send(labels.at[target[0]], label_in.at[k], label_send.at[k], label_recv.at[k], target)

    for h in (0, 1):
        for step in (1, -1):
            leg_one[h, step].wait_recv()
            tile = 2 * h + (step == -1)
            leg_one_on[h, step] = pass_amps(index(moved(h, here, -step)), (tile,), h, step)
            second_leg(h, step)
    leg_two_on = []

    def second_leg_on(h, b):
        for step in (1, -1):
            leg_two[h, b, step].wait_recv()
            tile = 2 * h + (step == -1)
            place = moved(1 - h, moved(h, here, -b), -step)
            leg_two_on.append(pass_amps(index(place), (tile,), 1 - h, step))

    for h in (0, 1):
        second_leg_on(h, 0)
    for h in (0, 1):
        for step in (1, -1):
            leg_one_on[h, step].wait_recv()
        second_leg(h, 2)
    tile_copies[SIBLING].wait_send()
    post(FAR[0], SIBLING)
    for b in (1, -1, 2):
        for h in (0, 1):
            second_leg_on(h, b)
    for k in range(7 if late else 0):
        target = across(k)

        @pl.loop(0, late)
        def _(t):
            outgoing_late[k, t] = stored[order[target[0] * CAP + early + t]]

    post_late(SIBLING)
    for k in NEAR:
        tile_copies[k].wait_send()
    post(FAR[1], NEAR[0])

    own_label.wait()
    for k in range(7):
        label_copies[k].wait()
    move = pltpu.make_async_copy(label_in, label_s, smem_sem)
    move.start()

    def tell(place, base, axis, step):
        return send(found.at[place], found.at[base], found_send.at[base - 1], found_recv.at[base - 1], along(axis, step))

    def tell_neighbours(place, axis):
        return tell(place, place + 1, axis, 1), tell(place, place + 2, axis, -1)

    def tell_on(place, axis, told):
        told[0].wait_recv()
        return tell(place + 1, place + 3, axis, 1)

    def add_up(place, told):
        told[0].wait_send()
        told[1].wait()
        told[2].wait()
        found[place + 4] = found[place] + found[place + 1] + found[place + 2] + found[place + 3]

    found[0] = jnp.sum(label_in[...], axis=0)
    told_y = tell_neighbours(0, 0)
    move.wait()
    own_amps.wait()
    for copy in leg_two_on:
        copy.wait_recv()
    for copy in sent:
        copy.wait_send()

    def contract(pairs, sources, opening, unroll=1):
        @pl.loop(0, MEMBERS // unroll)
        def _(turn):
            for d in [turn * unroll + u for u in range(unroll)]:
                for pair in pairs:
                    left, right = [], []
                    for k in sources:
                        for j in range(MEET):
                            entry = label_s[k, 0, pair * 64 + d * MEET + j]
                            row = entry & 255
                            tile = arrived[k][jnp.minimum(row, integrals.shape[0] - 1 if k == OWN else early - 1)]
                            if late and pair == 1 and k != OWN:
                                other = arrived_late[k][jnp.clip(row - early, 0, late - 1)]
                                tile = jnp.where(row < early, tile, other)
                            source = lax.shift_right_logical(entry, 8) & 63
                            column = lax.shift_right_logical(entry, 16)
                            left.append(block_amps[source // TILES, source & 3])
                            none = jnp.zeros_like(tile)
                            right.append(
                                jnp.concatenate([jnp.where(column == 0, tile, none), jnp.where(column == 1, tile, none)], axis=1)
                            )
                    product = jnp.dot(
                        jnp.concatenate(left, axis=1), jnp.concatenate(right, axis=0), preferred_element_type=jnp.float32
                    )
                    if opening:
                        totals[pair][d] = product
                    else:
                        totals[pair][d] += product

    tile_copies[SIBLING].wait_recv()
    contract((0,), (OWN, SIBLING), True, 2)
    told_y += (tell_on(0, 0, told_y),)
    for k in NEAR:
        tile_copies[k].wait_recv()
    contract((0,), NEAR, False, 2)
    add_up(0, told_y)
    told_z = tell_neighbours(4, 1)
    tile_copies[FAR[0]].wait()
    contract((0,), FAR[:1], False, 4)
    tile_copies[FAR[1]].wait()
    for k in NEAR:
        post_late(k)
    contract((0,), FAR[1:], False, 4)
    sums[0].code()
    sums[0].start_far()
    await_late(SIBLING)
    contract((1,), (OWN, SIBLING), True, 2)
    sums[0].start_near()
    told_z += (tell_on(4, 1, told_z),)
    for k in FAR:
        post_late(k)
    sums[0].relay()
    for k in NEAR:
        await_late(k)
    contract((1,), NEAR, False, 2)
    for k in FAR:
        await_late(k)
    contract((1,), FAR, False, 2)
    sums[1].code()
    sums[1].start_far()
    sums[0].turn()
    sums[1].start_near()
    sums[0].pass_on()
    sums[1].relay()
    sums[0].finish()
    sums[1].turn()
    sums[1].pass_on()
    add_up(4, told_z)
    report = pltpu.make_async_copy(found.at[8], excess, local_sem.at[0])
    report.start()
    sums[1].finish()
    report.wait()
    sums[0].close()
    sums[1].close()


def ladder(early, order, labels, integrals, amps):
    dma = pltpu.SemaphoreType.DMA
    late = CAP - early
    tiles = [pltpu.VMEM((7, late, W, W), jnp.bfloat16)] + [pltpu.VMEM((late, W, W), jnp.bfloat16)] * 7
    return pl.pallas_call(
        functools.partial(ladder_kernel, early),
        out_shape=(
            jax.ShapeDtypeStruct((TILES, ROWS, W), jnp.float32),
            jax.ShapeDtypeStruct((8, 128), jnp.int32),
        ),
        in_specs=[SMEM, ANY, ANY, ANY],
        out_specs=(ANY, ANY),
        scratch_shapes=[
            pltpu.VMEM(integrals.shape, jnp.bfloat16),
            pltpu.VMEM((len(FIRST), early, W, W), jnp.bfloat16),
            pltpu.VMEM((MEMBERS, TILES, ROWS, W), jnp.bfloat16),
            pltpu.VMEM((GROUPS, 8, 128), jnp.int32),
            pltpu.SMEM((GROUPS, 8, 128), jnp.int32),
            pltpu.VMEM((MEMBERS, ROWS, 2 * W), jnp.float32),
            pltpu.VMEM((MEMBERS, ROWS, 2 * W), jnp.float32),
        ]
        + [pltpu.VMEM((early, W, W), jnp.bfloat16)] * 7
        + (tiles if late else [])
        + [pltpu.VMEM((9, 8, 128), jnp.int32), dma((7,)), dma((7,))]
        + [dma((7,)), dma((7,)), dma((7,)), dma((7,)), dma((7,)), dma((7,)), dma((40,)), dma((40,)), dma((3,)), dma]
        + reduce_scratch() * 2,
        compiler_params=pltpu.CompilerParams(collective_id=0 if late else 1, has_side_effects=True, vmem_limit_bytes=60 << 20),
        name="ladder" if late else "ladder_at_once",
    )(order, labels, integrals, amps)


def slots(plan):
    rows = plan.shape[0]
    group = plan[:, 2] // MEMBERS
    source = plan[:, 0] % BLOCK
    target = plan[:, 1] % BLOCK
    tile = target % TILES
    row = jnp.arange(rows, dtype=jnp.int32)
    before = row[None, :] < row[:, None]
    here = group[None, :] == group[:, None]
    pair = tile // 2
    ahead = (pair[None, :] < pair[:, None]) | ((pair[None, :] == pair[:, None]) & before)
    slot = jnp.sum((here & ahead).astype(jnp.int32), axis=1)
    meet = group * 128 + pair * 64 + (target // TILES) * MEET
    place = meet + jnp.sum(((meet[None, :] == meet[:, None]) & before).astype(jnp.int32), axis=1)
    stay = group == lax.axis_index("group")
    entry = jnp.where(stay, row, slot) + 256 * source + 65536 * (tile % 2)
    at = jnp.arange(GROUPS * CAP, dtype=jnp.int32)[:, None] == (group * CAP + slot)[None, :]
    order = jnp.sum(jnp.where(at, row[None, :], 0), axis=1)
    at = jnp.arange(GROUPS * 128, dtype=jnp.int32)[:, None] == place[None, :]
    labels = 2 * 65536 + jnp.sum(jnp.where(at, entry[None, :] - 2 * 65536, 0), axis=1)
    over = jnp.sum(((pair == 0) & (slot >= EARLY) & ~stay).astype(jnp.int32))
    labels = jnp.where(jnp.arange(8, dtype=jnp.int32)[None, :, None] == 0, labels.reshape(GROUPS, 1, 128), over)
    return order, labels


def on_device(amplitudes, integrals, task_plan):
    order, labels = slots(task_plan)
    out, excess = ladder(EARLY, order, labels, integrals, amplitudes)

    def all_early():
        return ladder(CAP, order, labels, integrals, amplitudes)[0]

    return lax.cond(excess[1, 0] > 0, all_early, lambda: out)


def solution(mesh):
    in_specs = (
        P(("group", "member"), None, None),
        P(("group", "member"), None, None),
        P(("group", "member"), None),
    )
    out_specs = P(("group", "member"), None, None)
    return jax.shard_map(
        on_device, mesh=mesh, in_specs=in_specs, out_specs=out_specs, check_vma=False
    )
```

```python
import functools

import jax
import jax.numpy as jnp
from jax import lax
from jax.experimental import pallas as pl
from jax.experimental.pallas import tpu as pltpu
from jax.sharding import PartitionSpec as P

MESH = pl.DeviceIdType.MESH
ANY = pl.BlockSpec(memory_space=pl.ANY)
VMEM = pl.BlockSpec(memory_space=pltpu.VMEM)
SMEM = pl.BlockSpec(memory_space=pltpu.SMEM)

NX, NC, NY, NZ = 4, 2, 4, 4
GROUPS = NX * NC
MEMBERS = NY * NZ
CAP = 32
TILES = 4
BLOCK = MEMBERS * TILES
MEET = 4
EARLY = 26
W = 128
ROWS = 512
HALF = ROWS // 2
CODED = HALF + 16

PEERS = ((1, 0), (3, 0), (1, 1), (3, 1), (0, 1), (2, 0), (2, 1))
NEAR, SIBLING, FAR, OWN = (0, 1, 2, 3), 4, (5, 6), 7
FIRST = NEAR + (SIBLING,)

CASES = tuple((h, w) for h in (0, 1) for w in (0, 1))


def wrap(value, size):
    return lax.rem(value + size, size)


def encode(value):
    blocks = value.reshape(HALF // 16, 16, W)
    most = jnp.max(jnp.abs(blocks), axis=0)
    power = jnp.ceil(jnp.log2(jnp.maximum(most, 1e-30)) - 14.999)
    whole = jnp.round(blocks * jnp.exp2(-power)[None]).astype(jnp.int32)
    return whole.reshape(HALF, W).astype(jnp.int16), power.astype(jnp.int32).astype(jnp.int16)


def decode(ref):
    factor = jnp.exp2(ref[pl.ds(HALF, 16), :].astype(jnp.int32).astype(jnp.float32))
    whole = ref[pl.ds(0, HALF), :].astype(jnp.int32).astype(jnp.float32)
    return (whole.reshape(HALF // 16, 16, W) * factor[None]).reshape(HALF, W)


def write(ref, value):
    whole, power = encode(value)
    ref[pl.ds(0, HALF), :] = whole
    ref[pl.ds(HALF, 16), :] = power


class Reduce:
    def __init__(self, at, along, pair, total, parts, bufs, sems, out):
        self.at, self.along, self.pair, self.total, self.parts, self.out = at, along, pair, total, parts, out
        self.a_in, self.b_in, self.c_in, self.d_in, self.e_in, self.f_in = bufs
        self.sems = sems
        self.copies = {}

    def second(self, i, k):
        h, w = CASES[i]
        sense = 1 - 2 * w
        return wrap(self.at[1 - h] + (2, -sense, sense, 0)[k], 4)

    def send(self, name, src, dst, leg, step, *index):
        send_sem, recv_sem = self.sems[name]
        key = index if len(index) > 1 else index[0]
        copy = pltpu.make_async_remote_copy(
            src_ref=src, dst_ref=dst, send_sem=send_sem.at[key], recv_sem=recv_sem.at[key],
            device_id=self.along(leg, step), device_id_type=MESH,
        )
        copy.start()
        self.copies[(name,) + index] = copy

    def own(self, i, q):
        h, w = CASES[i]
        d = self.at[0] * NZ + q if h == 0 else q * NZ + self.at[1]
        return self.total.at[d, pl.ds(h * HALF, HALF), pl.ds(w * W, W)]

    def code(self):
        @pl.loop(0, 12)
        def _(t):
            r, q = t // 4, lax.rem(t, 4)
            for h, w in CASES:
                p = wrap(self.at[h] + r + 1, 4)
                d = p * NZ + q if h == 0 else q * NZ + p
                write(self.parts.at[h, w, r, q], self.total[d, pl.ds(h * HALF, HALF), pl.ds(w * W, W)])

    def start_far(self):
        for k in range(4):
            for i, (h, w) in enumerate(CASES):
                sense = 1 - 2 * w
                self.send(
                    "a", self.parts.at[h, w, 1, self.second(i, k)], self.a_in.at[i, k], h, sense, i, k
                )

    def start_near(self):
        for i, (h, w) in enumerate(CASES):
            sense = 1 - 2 * w
            self.send("b", self.parts.at[h, w, 1 + sense], self.b_in.at[i], h, -sense, i)

    def relay(self):
        for k in range(4):
            for i, (h, w) in enumerate(CASES):
                sense = 1 - 2 * w
                self.copies["a", i, k].wait()
                own = self.parts.at[h, w, 1 - sense, self.second(i, k)]
                write(self.a_in.at[i, k], decode(self.a_in.at[i, k]) + decode(own))
                self.send("c", self.a_in.at[i, k], self.c_in.at[i, k], h, sense, i, k)

    def turn(self):
        for i in range(4):
            self.copies["b", i].wait()
        for k in range(4):
            for i, (h, w) in enumerate(CASES):
                sense = 1 - 2 * w
                q = self.second(i, k)
                self.copies["c", i, k].wait()
                value = decode(self.c_in.at[i, k]) + self.own(i, q)[...] + decode(self.b_in.at[i, q])
                if k == 0:
                    write(self.a_in.at[i, 0], value)
                    self.send("d", self.a_in.at[i, 0], self.d_in.at[i], 1 - h, sense, i)
                elif k == 1:
                    write(self.a_in.at[i, 1], value)
                    self.send("e", self.a_in.at[i, 1], self.e_in.at[i], 1 - h, -sense, i)
                else:
                    self.own(i, q)[...] = value

    def pass_on(self):
        for i, (h, w) in enumerate(CASES):
            sense = 1 - 2 * w
            self.copies["d", i].wait()
            write(self.d_in.at[i], decode(self.d_in.at[i]) + self.own(i, self.second(i, 2))[...])
            self.send("f", self.d_in.at[i], self.f_in.at[i], 1 - h, sense, i)

    def finish(self):
        for i, (h, w) in enumerate(CASES):
            self.copies["e", i].wait()
            self.copies["f", i].wait()
            own = self.own(i, self.second(i, 3))
            own[...] = own[...] + decode(self.e_in.at[i]) + decode(self.f_in.at[i])
            self.copies["out", i] = pltpu.make_async_copy(
                own, self.out.at[2 * self.pair + w, pl.ds(h * HALF, HALF)], self.sems["out"].at[i]
            )
            self.copies["out", i].start()

    def close(self):
        for i in range(4):
            self.copies["out", i].wait()


REDUCE_SEMS = (("a", (4, 4)), ("b", (4,)), ("c", (4, 4)), ("d", (4,)), ("e", (4,)), ("f", (4,)))


def reduce_scratch():
    tile = (CODED, W)
    shapes = [
        pltpu.VMEM((2, 2, 3, 4) + tile, jnp.int16),
        pltpu.VMEM((4, 4) + tile, jnp.int16),
        pltpu.VMEM((4, 4) + tile, jnp.int16),
        pltpu.VMEM((4, 4) + tile, jnp.int16),
        pltpu.VMEM((4,) + tile, jnp.int16),
        pltpu.VMEM((4,) + tile, jnp.int16),
        pltpu.VMEM((4,) + tile, jnp.int16),
    ]
    for _, shape in REDUCE_SEMS:
        shapes += [pltpu.SemaphoreType.DMA(shape)] * 2
    return shapes + [pltpu.SemaphoreType.DMA((4,))]


def ladder_kernel(early, order, labels, integrals, amps, out, excess, *scratch):
    scratch = list(scratch)
    late = CAP - early

    def take(n):
        taken = scratch[:n]
        del scratch[:n]
        return taken

    stored, outgoing, block_amps, label_in, label_s, *totals = take(7)
    arrived = take(7) + [stored]
    if late:
        outgoing_late, *arrived_late = take(8)
    found, found_send, found_recv = take(3)
    tile_send, tile_recv, late_send, late_recv, label_send, label_recv, amp_send, amp_recv, local_sem, smem_sem = take(10)

    group = lax.axis_index("group")
    member = lax.axis_index("member")
    x, core, y, z = group // NC, lax.rem(group, NC), member // NZ, lax.rem(member, NZ)

    def across(k):
        dx, dc = PEERS[k]
        return (wrap(x + dx, NX) * NC + wrap(core + dc, NC), member)

    def along(axis, step):
        if axis == 0:
            return (group, wrap(y + step, NY) * NZ + z)
        return (group, y * NZ + wrap(z + step, NZ))

    sums = []
    for pair in (0, 1):
        parts, *bufs = take(7)
        sems = {name: tuple(take(2)) for name, _ in REDUCE_SEMS}
        (sems["out"],) = take(1)
        sums.append(Reduce((y, z), along, pair, totals[pair], parts, bufs, sems, out))

    load = pltpu.make_async_copy(integrals, stored, local_sem.at[0])
    load.start()
    own_amps = pltpu.make_async_copy(amps, block_amps.at[member], local_sem.at[1])
    own_amps.start()
    own_label = pltpu.make_async_copy(labels.at[group], label_in.at[OWN], local_sem.at[2])
    own_label.start()

    barrier = pltpu.get_barrier_semaphore()
    for k in range(7):
        pl.semaphore_signal(barrier, inc=1, device_id=across(k), device_id_type=MESH)
    for axis in (0, 1):
        for step in (1, -1):
            pl.semaphore_signal(barrier, inc=1, device_id=along(axis, step), device_id_type=MESH)
    pl.semaphore_wait(barrier, 11)

    def send(src, dst, send_sem, recv_sem, target):
        copy = pltpu.make_async_remote_copy(
            src_ref=src, dst_ref=dst, send_sem=send_sem, recv_sem=recv_sem, device_id=target, device_id_type=MESH
        )
        copy.start()
        return copy

    sent = []

    def pass_amps(where, tiles, axis, step):
        count = len(sent)
        ref = block_amps.at[where, pl.ds(tiles[0], len(tiles))]
        source = amps.at[pl.ds(tiles[0], len(tiles))] if where is member else ref
        copy = send(source, ref, amp_send.at[count], amp_recv.at[count], along(axis, step))
        sent.append(copy)
        return copy

    def moved(axis, place, step):
        a, b = place
        return (wrap(a + step, 4), b) if axis == 0 else (a, wrap(b + step, 4))

    def index(place):
        return place[0] * NZ + place[1]

    here = (y, z)
    leg_one = {}
    for h in (0, 1):
        for step in (1, -1):
            leg_one[h, step] = pass_amps(member, (2 * h, 2 * h + 1), h, step)

    leg_two, leg_one_on = {}, {}

    def second_leg(h, b):
        where = member if b == 0 else index(moved(h, here, -b))
        for step in (1, -1):
            leg_two[h, b, step] = pass_amps(where, (2 * h, 2 * h + 1), 1 - h, step)

    for h in (0, 1):
        second_leg(h, 0)

    load.wait()
    tile_copies, label_copies = {}, {}

    def post(k, slot):
        target = across(k)

        @pl.loop(0, early)
        def _(t):
            outgoing[slot, t] = stored[order[target[0] * CAP + t]]

        tile_copies[k] = send(outgoing.at[slot], arrived[k], tile_send.at[k], tile_recv.at[k], target)

    late_copies = {}

    def post_late(k):
        if late:
            late_copies[k] = send(
                outgoing_late.at[k], arrived_late[k], late_send.at[k], late_recv.at[k], across(k)
            )

    def await_late(k):
        if late:
            late_copies[k].wait()

    for k in FIRST:
        post(k, k)
    for k in range(7):
        target = across(k)
        label_copies[k] = send(labels.at[target[0]], label_in.at[k], label_send.at[k], label_recv.at[k], target)

    for h in (0, 1):
        for step in (1, -1):
            leg_one[h, step].wait_recv()
            tile = 2 * h + (step == -1)
            leg_one_on[h, step] = pass_amps(index(moved(h, here, -step)), (tile,), h, step)
            second_leg(h, step)
    leg_two_on = []

    def second_leg_on(h, b):
        for step in (1, -1):
            leg_two[h, b, step].wait_recv()
            tile = 2 * h + (step == -1)
            place = moved(1 - h, moved(h, here, -b), -step)
            leg_two_on.append(pass_amps(index(place), (tile,), 1 - h, step))

    for h in (0, 1):
        second_leg_on(h, 0)
    for h in (0, 1):
        for step in (1, -1):
            leg_one_on[h, step].wait_recv()
        second_leg(h, 2)
    tile_copies[SIBLING].wait_send()
    post(FAR[0], SIBLING)
    for b in (1, -1, 2):
        for h in (0, 1):
            second_leg_on(h, b)
    for k in range(7 if late else 0):
        target = across(k)

        @pl.loop(0, late)
        def _(t):
            outgoing_late[k, t] = stored[order[target[0] * CAP + early + t]]

    post_late(SIBLING)
    for k in NEAR:
        tile_copies[k].wait_send()
    post(FAR[1], NEAR[0])

    own_label.wait()
    for k in range(7):
        label_copies[k].wait()
    move = pltpu.make_async_copy(label_in, label_s, smem_sem)
    move.start()

    def tell(place, base, axis, step):
        return send(found.at[place], found.at[base], found_send.at[base - 1], found_recv.at[base - 1], along(axis, step))

    def tell_neighbours(place, axis):
        return tell(place, place + 1, axis, 1), tell(place, place + 2, axis, -1)

    def tell_on(place, axis, told):
        told[0].wait_recv()
        return tell(place + 1, place + 3, axis, 1)

    def add_up(place, told):
        told[0].wait_send()
        told[1].wait()
        told[2].wait()
        found[place + 4] = found[place] + found[place + 1] + found[place + 2] + found[place + 3]

    found[0] = jnp.sum(label_in[...], axis=0)
    told_y = tell_neighbours(0, 0)
    move.wait()
    own_amps.wait()
    for copy in leg_two_on:
        copy.wait_recv()
    for copy in sent:
        copy.wait_send()

    def contract(pairs, sources, opening, unroll=1):
        @pl.loop(0, MEMBERS // unroll)
        def _(turn):
            for d in [turn * unroll + u for u in range(unroll)]:
                for pair in pairs:
                    left, right = [], []
                    for k in sources:
                        for j in range(MEET):
                            entry = label_s[k, 0, pair * 64 + d * MEET + j]
                            row = entry & 255
                            tile = arrived[k][jnp.minimum(row, integrals.shape[0] - 1 if k == OWN else early - 1)]
                            if late and pair == 1 and k != OWN:
                                other = arrived_late[k][jnp.clip(row - early, 0, late - 1)]
                                tile = jnp.where(row < early, tile, other)
                            source = lax.shift_right_logical(entry, 8) & 63
                            column = lax.shift_right_logical(entry, 16)
                            left.append(block_amps[source // TILES, source & 3])
                            none = jnp.zeros_like(tile)
                            right.append(
                                jnp.concatenate([jnp.where(column == 0, tile, none), jnp.where(column == 1, tile, none)], axis=1)
                            )
                    product = jnp.dot(
                        jnp.concatenate(left, axis=1), jnp.concatenate(right, axis=0), preferred_element_type=jnp.float32
                    )
                    if opening:
                        totals[pair][d] = product
                    else:
                        totals[pair][d] += product

    tile_copies[SIBLING].wait_recv()
    contract((0,), (OWN, SIBLING), True, 2)
    told_y += (tell_on(0, 0, told_y),)
    for k in NEAR:
        tile_copies[k].wait_recv()
    contract((0,), NEAR, False, 2)
    add_up(0, told_y)
    told_z = tell_neighbours(4, 1)
    tile_copies[FAR[0]].wait()
    contract((0,), FAR[:1], False, 4)
    tile_copies[FAR[1]].wait()
    for k in NEAR:
        post_late(k)
    contract((0,), FAR[1:], False, 4)
    sums[0].code()
    sums[0].start_far()
    await_late(SIBLING)
    contract((1,), (OWN, SIBLING), True, 2)
    sums[0].start_near()
    told_z += (tell_on(4, 1, told_z),)
    sums[0].relay()
    for k in FAR:
        post_late(k)
    for k in NEAR:
        await_late(k)
    contract((1,), NEAR, False, 2)
    for k in FAR:
        await_late(k)
    contract((1,), FAR, False, 2)
    sums[1].code()
    sums[1].start_far()
    sums[0].turn()
    sums[1].start_near()
    sums[0].pass_on()
    sums[1].relay()
    sums[0].finish()
    sums[1].turn()
    sums[1].pass_on()
    add_up(4, told_z)
    report = pltpu.make_async_copy(found.at[8], excess, local_sem.at[0])
    report.start()
    sums[1].finish()
    report.wait()
    sums[0].close()
    sums[1].close()


def ladder(early, order, labels, integrals, amps):
    dma = pltpu.SemaphoreType.DMA
    late = CAP - early
    tiles = [pltpu.VMEM((7, late, W, W), jnp.bfloat16)] + [pltpu.VMEM((late, W, W), jnp.bfloat16)] * 7
    return pl.pallas_call(
        functools.partial(ladder_kernel, early),
        out_shape=(
            jax.ShapeDtypeStruct((TILES, ROWS, W), jnp.float32),
            jax.ShapeDtypeStruct((8, 128), jnp.int32),
        ),
        in_specs=[SMEM, ANY, ANY, ANY],
        out_specs=(ANY, ANY),
        scratch_shapes=[
            pltpu.VMEM(integrals.shape, jnp.bfloat16),
            pltpu.VMEM((len(FIRST), early, W, W), jnp.bfloat16),
            pltpu.VMEM((MEMBERS, TILES, ROWS, W), jnp.bfloat16),
            pltpu.VMEM((GROUPS, 8, 128), jnp.int32),
            pltpu.SMEM((GROUPS, 8, 128), jnp.int32),
            pltpu.VMEM((MEMBERS, ROWS, 2 * W), jnp.float32),
            pltpu.VMEM((MEMBERS, ROWS, 2 * W), jnp.float32),
        ]
        + [pltpu.VMEM((early, W, W), jnp.bfloat16)] * 7
        + (tiles if late else [])
        + [pltpu.VMEM((9, 8, 128), jnp.int32), dma((7,)), dma((7,))]
        + [dma((7,)), dma((7,)), dma((7,)), dma((7,)), dma((7,)), dma((7,)), dma((40,)), dma((40,)), dma((3,)), dma]
        + reduce_scratch() * 2,
        compiler_params=pltpu.CompilerParams(collective_id=0 if late else 1, has_side_effects=True, vmem_limit_bytes=60 << 20),
        name="ladder" if late else "ladder_at_once",
    )(order, labels, integrals, amps)


def slots(plan):
    rows = plan.shape[0]
    group = plan[:, 2] // MEMBERS
    source = plan[:, 0] % BLOCK
    target = plan[:, 1] % BLOCK
    tile = target % TILES
    row = jnp.arange(rows, dtype=jnp.int32)
    before = row[None, :] < row[:, None]
    here = group[None, :] == group[:, None]
    pair = tile // 2
    ahead = (pair[None, :] < pair[:, None]) | ((pair[None, :] == pair[:, None]) & before)
    slot = jnp.sum((here & ahead).astype(jnp.int32), axis=1)
    meet = group * 128 + pair * 64 + (target // TILES) * MEET
    place = meet + jnp.sum(((meet[None, :] == meet[:, None]) & before).astype(jnp.int32), axis=1)
    stay = group == lax.axis_index("group")
    entry = jnp.where(stay, row, slot) + 256 * source + 65536 * (tile % 2)
    at = jnp.arange(GROUPS * CAP, dtype=jnp.int32)[:, None] == (group * CAP + slot)[None, :]
    order = jnp.sum(jnp.where(at, row[None, :], 0), axis=1)
    at = jnp.arange(GROUPS * 128, dtype=jnp.int32)[:, None] == place[None, :]
    labels = 2 * 65536 + jnp.sum(jnp.where(at, entry[None, :] - 2 * 65536, 0), axis=1)
    over = jnp.sum(((pair == 0) & (slot >= EARLY) & ~stay).astype(jnp.int32))
    labels = jnp.where(jnp.arange(8, dtype=jnp.int32)[None, :, None] == 0, labels.reshape(GROUPS, 1, 128), over)
    return order, labels


def on_device(amplitudes, integrals, task_plan):
    order, labels = slots(task_plan)
    out, excess = ladder(EARLY, order, labels, integrals, amplitudes)

    def all_early():
        return ladder(CAP, order, labels, integrals, amplitudes)[0]

    return lax.cond(excess[1, 0] > 0, all_early, lambda: out)


def solution(mesh):
    in_specs = (
        P(("group", "member"), None, None),
        P(("group", "member"), None, None),
        P(("group", "member"), None),
    )
    out_specs = P(("group", "member"), None, None)
    return jax.shard_map(
        on_device, mesh=mesh, in_specs=in_specs, out_specs=out_specs, check_vma=False
    )
```
